32 devices in a mesh: parts: 2 (over y), row: 4 (over z), col: 4 (over x, core).
Axes of the slice: x: 2, y: 2, z: 4, core: 2. Of those that a mesh axis runs over, the one named last changes fastest.
Arguments:
- pair: float32 [192, 96, 128], P(('parts', 'row'), 'col'), parts along dimension 0, may hold values from -6 to 6
- chain: int32 [192], P('parts'), parts along dimension 0, may hold values from 0 to 3, never falling along the last dimension, each value on 1 to 48 neighbouring positions
- block_mask: int32 [24, 12], P('parts'), parts along dimension 0, may hold values 0 or 1
- norm_gain: float32 [5, 128], replicated, may hold values from 0.1 to 1.9
- norm_bias: float32 [5, 128], replicated, may hold values from -3 to 3
- w_proj: bfloat16 [2, 128, 640], replicated, may hold values from -0.5 to 0.5
- w_out: bfloat16 [2, 128, 128], replicated, may hold values from -0.5 to 0.5
- w_trans_in: bfloat16 [128, 1024], replicated, may hold values from -0.5 to 0.5
- w_trans_out: bfloat16 [512, 128], replicated, may hold values from -0.25 to 0.25
Outputs:
- pair_out: float32 [192, 96, 128], P(('parts', 'row'), 'col'), parts along dimension 0
The draws below stay inside these ranges and needn't reach their ends.
There are 2 independent parts, one for each index of `parts`. The reference program is written for one: setup_inputs(seed, part) draws one part's arguments, and reference() takes and returns one part's arrays. A program takes and returns all parts, laid end to end along the dimension named above; an argument that names none is the same for every part. Nothing has to cross between parts.
Inputs may be any that keep to these rules, and one draw needn't show every extreme that they name: Chain ids never fall along the residues; one chain has exactly 48 residues and none has more.
All inputs are finite; a program needn't handle non-finite values.
Results may differ from the reference program's by a relative error of at most 0.0057.
Values may be sent and summed in bfloat16 or wider, within the bound.
A program may use at most 64 MiB of HBM per device.

```python
import math
import jax
import jax.numpy as jnp
import numpy as np
from jax import lax

CHAN = 128
HID = 512
MASK_TILE = 8
N_RES = 96


def place_ends(array, rng, least, largest):
    dims = array.shape
    spot = [jax.random.randint(jax.random.fold_in(rng, axis), (), 0, dims[axis]) for axis in range(len(dims))]
    array = array.at[tuple(spot)].set(least)
    longest = dims.index(max(dims))
    spot[longest] = (spot[longest] + 1) % dims[longest]
    return array.at[tuple(spot)].set(largest)


def steps_of(stream_key, shape, cuts, low, top_value):
    factor_of = 1.0
    for position, shards_of in cuts:
        steps = jax.random.uniform(jax.random.fold_in(jax.random.fold_in(stream_key, 6), position), (shards_of,), jnp.float32, low / len(cuts), top_value / len(cuts))
        factor_of = factor_of * jnp.repeat(jnp.exp(steps), shape[position] // shards_of).reshape((-1,) + (1,) * (len(shape) - 1 - position))
    return factor_of


def split_up(count, total, limit, lean):
    loads = [(1 << 20) // math.isqrt(grade ** lean) + 1 for grade in range(2, count + 1)]
    surplus, counts = total - limit - (count - 1), [1] * (count - 1)
    while surplus > 0:
        free = [i for i in range(count - 1) if counts[i] < limit]
        mass, budget = sum([loads[i] for i in free]), surplus
        for i in free:
            more = min(limit - counts[i], max(1, budget * loads[i] // mass), surplus)
            counts[i] = counts[i] + more
            surplus = surplus - more
    return np.array([limit] + counts)


def uneven_parts(own_key, amount, total, bound, lean):
    if amount == 2:
        one = jax.random.randint(own_key, (), max(1, total - bound), min(bound, total - 1) + 1)
        return jnp.stack([one, total - one])
    lengths = jnp.asarray(split_up(amount, total, bound, lean), jnp.int32)
    twos = (amount - 1) // 2
    donor, taker = lengths[1:1 + 2 * twos:2], lengths[2:2 + 2 * twos:2]
    slack = jnp.minimum(donor - 1, bound - taker)
    moved = jax.random.randint(jax.random.fold_in(own_key, 1), (twos,), 0, 1 << 20) % (slack + 1)
    lengths = lengths.at[1:1 + 2 * twos:2].set(donor - moved).at[2:2 + 2 * twos:2].set(taker + moved)
    return lengths[jax.random.permutation(jax.random.fold_in(own_key, 2), amount)]


def noise(stream_key, shape, scale, most, cuts=(), kind=jnp.bfloat16):
    drawn = scale * jax.random.normal(stream_key, shape, jnp.float32)
    if cuts:
        drawn = drawn * steps_of(stream_key, shape, cuts, -0.22, 0.18)
    return jnp.clip(drawn, -most, most).astype(kind)


def setup_inputs(seed: int = 0, part: int = 0) -> dict:
    splits = jax.random.split(jax.random.key(seed), 10)
    own_keys = jax.random.split(jax.random.fold_in(splits[9], part), 10)
    pair = noise(own_keys[0], (N_RES, N_RES, CHAN), 1.0, 6.0, ((0, 4), (1, 4)), jnp.float32)
    chain = jnp.searchsorted(jnp.cumsum(uneven_parts(own_keys[1], 4, N_RES, N_RES // 2, 0)), jnp.arange(N_RES), side="right").astype(jnp.int32)
    block_mask = place_ends((jax.random.randint(own_keys[2], (N_RES // MASK_TILE, N_RES // MASK_TILE), 0, 2) < 1).astype(jnp.int32), jax.random.fold_in(own_keys[2], 1), 0, 1)
    norm_gain = jnp.clip(1.0 + 0.18 * jax.random.normal(splits[3], (5, CHAN), jnp.float32), 0.1, 1.9)
    norm_bias = noise(splits[4], (5, CHAN), 0.5, 3.0, (), jnp.float32)
    w_proj = noise(splits[5], (2, CHAN, 5 * CHAN), CHAN ** -0.5, 0.5)
    w_out = noise(splits[6], (2, CHAN, CHAN), CHAN ** -0.5, 0.5)
    w_trans_in = noise(splits[7], (CHAN, 2 * HID), CHAN ** -0.5, 0.5)
    w_trans_out = noise(splits[8], (HID, CHAN), HID ** -0.5, 0.25)
    return dict(pair=pair, chain=chain, block_mask=block_mask, norm_gain=norm_gain, norm_bias=norm_bias, w_proj=w_proj, w_out=w_out, w_trans_in=w_trans_in, w_trans_out=w_trans_out)


def layer_norm(values, gain, bias):
    center = lax.optimization_barrier(jnp.mean(values, axis=-1, keepdims=True))
    spread = lax.optimization_barrier(jnp.mean((values - center) ** 2, axis=-1, keepdims=True))
    return (values - center) * lax.rsqrt(spread + 1e-05) * gain + bias

def reference(pair, chain, block_mask, norm_gain, norm_bias, w_proj, w_out, w_trans_in, w_trans_out):
    same_chain = chain[:, None] == chain[None, :]
    expanded = jnp.repeat(jnp.repeat(block_mask, MASK_TILE, axis=0), MASK_TILE, axis=1) > 0
    pair_mask = jnp.logical_or(same_chain, expanded).astype(jnp.float32)[..., None]
    state = pair
    for update in range(2):
        normed = layer_norm(state, norm_gain[2 * update], norm_bias[2 * update]).astype(jnp.bfloat16)
        proj = jnp.dot(normed, w_proj[update], preferred_element_type=jnp.float32)
        left_edge = (jax.nn.sigmoid(proj[..., 0:CHAN]) * proj[..., CHAN:2 * CHAN] * pair_mask).astype(jnp.bfloat16)
        right_edge = (jax.nn.sigmoid(proj[..., 2 * CHAN:3 * CHAN]) * proj[..., 3 * CHAN:4 * CHAN] * pair_mask).astype(jnp.bfloat16)
        gating = jax.nn.sigmoid(proj[..., 4 * CHAN:])
        left_wide = left_edge.astype(jnp.float32)
        right_wide = right_edge.astype(jnp.float32)
        if update == 0:
            triangle = jnp.einsum('ikc,jkc->ijc', left_wide, right_wide, precision=lax.Precision.HIGHEST)
        else:
            triangle = jnp.einsum('kic,kjc->ijc', left_wide, right_wide, precision=lax.Precision.HIGHEST)
        tri_norm = layer_norm(triangle, norm_gain[2 * update + 1], norm_bias[2 * update + 1]).astype(jnp.bfloat16)
        state = state + gating * jnp.dot(tri_norm, w_out[update], preferred_element_type=jnp.float32)
    trans_norm = layer_norm(state, norm_gain[4], norm_bias[4]).astype(jnp.bfloat16)
    hidden_pre = jnp.dot(trans_norm, w_trans_in, preferred_element_type=jnp.float32)
    activated = (jax.nn.silu(hidden_pre[..., :HID]) * hidden_pre[..., HID:]).astype(jnp.bfloat16)
    return state + jnp.dot(activated, w_trans_out, preferred_element_type=jnp.float32)
```

```python
import functools

import jax
import jax.numpy as jnp
from jax import lax
from jax.experimental import pallas as pl
from jax.experimental.pallas import tpu as pltpu
from jax.sharding import PartitionSpec as P

MASK_TILE = 8
MESH = pl.DeviceIdType.MESH


def broadcast(array, axis, root):
    mine = lax.axis_index(axis) == root
    return lax.psum(jnp.where(mine, array, jnp.zeros_like(array)), axis)


def layer_norm(values, gain, bias):
    center = jnp.mean(values, axis=-1, keepdims=True)
    spread = jnp.mean((values - center) ** 2, axis=-1, keepdims=True)
    return (values - center) * lax.rsqrt(spread + 1e-05) * gain + bias


def project_edges(state, pair_mask, norm_gain, norm_bias, w_proj, update):
    channels = state.shape[2]
    normed = layer_norm(state, norm_gain[2 * update], norm_bias[2 * update]).astype(jnp.bfloat16)
    proj = jnp.dot(normed, w_proj[update], preferred_element_type=jnp.float32)
    left_edge = (
        jax.nn.sigmoid(proj[..., 0:channels]) * proj[..., channels : 2 * channels] * pair_mask
    ).astype(jnp.bfloat16)
    right_edge = (
        jax.nn.sigmoid(proj[..., 2 * channels : 3 * channels])
        * proj[..., 3 * channels : 4 * channels]
        * pair_mask
    ).astype(jnp.bfloat16)
    gating = jax.nn.sigmoid(proj[..., 4 * channels :])
    return (left_edge, right_edge, gating)


def finish_update(state, triangle, gating, norm_gain, norm_bias, w_out, update):
    tri_norm = layer_norm(triangle, norm_gain[2 * update + 1], norm_bias[2 * update + 1]).astype(
        jnp.bfloat16
    )
    return state + gating * jnp.dot(tri_norm, w_out[update], preferred_element_type=jnp.float32)


def local(pair, chain, block_mask, norm_gain, norm_bias, w_proj, w_out, w_trans_in, w_trans_out):
    extent = pair.shape[0]
    row_offset = lax.axis_index("row") * extent
    col_offset = lax.axis_index("col") * extent
    row_chain = lax.dynamic_slice_in_dim(chain, row_offset, extent)
    col_chain = lax.dynamic_slice_in_dim(chain, col_offset, extent)
    expanded = jnp.repeat(jnp.repeat(block_mask, MASK_TILE, axis=0), MASK_TILE, axis=1)
    local_blocks = lax.dynamic_slice(expanded, (row_offset, col_offset), (extent, extent)) > 0
    same_chain = row_chain[:, None] == col_chain[None, :]
    pair_mask = jnp.logical_or(same_chain, local_blocks).astype(jnp.float32)[..., None]
    state = pair
    left_edge, right_edge, gating = project_edges(state, pair_mask, norm_gain, norm_bias, w_proj, 0)
    right_strip = lax.all_gather(right_edge, "col", axis=1, tiled=True)
    mirrored_right = broadcast(right_strip, "row", lax.axis_index("col"))
    partner = mirrored_right
    triangle = jnp.einsum(
        "ikc,jkc->ijc",
        lax.all_gather(left_edge, "col", axis=1, tiled=True),
        partner,
        preferred_element_type=jnp.float32,
    )
    state = finish_update(state, triangle, gating, norm_gain, norm_bias, w_out, 0)
    left_edge, right_edge, gating = project_edges(state, pair_mask, norm_gain, norm_bias, w_proj, 1)
    left_strip = lax.all_gather(left_edge, "row", axis=0, tiled=True)
    mirrored_left = broadcast(left_strip, "col", lax.axis_index("row"))
    partner = mirrored_left
    triangle = jnp.einsum(
        "kic,kjc->ijc",
        partner,
        lax.all_gather(right_edge, "row", axis=0, tiled=True),
        preferred_element_type=jnp.float32,
    )
    state = finish_update(state, triangle, gating, norm_gain, norm_bias, w_out, 1)
    trans_norm = layer_norm(state, norm_gain[4], norm_bias[4]).astype(jnp.bfloat16)
    hidden_pre = jnp.dot(trans_norm, w_trans_in, preferred_element_type=jnp.float32)
    width = w_trans_out.shape[0]
    activated = (jax.nn.silu(hidden_pre[..., :width]) * hidden_pre[..., width:]).astype(
        jnp.bfloat16
    )
    return state + jnp.dot(activated, w_trans_out, preferred_element_type=jnp.float32)


GROUPS = 16
WIDTH = 8
SIDE = 24
LR_ROWS = 80
TRI_ROWS = 48


def sigmoid(x):
    return 0.5 * jnp.tanh(0.5 * x) + 0.5


def swap_groups(values, lane):
    values = list(values)
    for step in (8, 4, 2, 1):
        low = (lane & (step * WIDTH)) == 0
        for a in range(GROUPS):
            if a & step:
                continue
            first, second = values[a], values[a + step]
            values[a] = jnp.where(low, first, pltpu.roll(second, step * WIDTH, 1))
            values[a + step] = jnp.where(low, pltpu.roll(first, 128 - step * WIDTH, 1), second)
    return values


def norm_rows(x, gain, bias):
    center = jnp.mean(x, axis=-1, keepdims=True)
    off = x - center
    spread = jnp.mean(off * off, axis=-1, keepdims=True)
    return (off * lax.rsqrt(spread + 1e-05) * gain + bias).astype(jnp.bfloat16)


def kernel(
    cols, pair, chain, block_mask, gain, bias, w_proj, w_out, w_in, w_down, out,
    edges, gates, state, tri, lr_out, lr_in, tri_out, tri_in, send_sem, recv_sem,
):
    row, col = lax.axis_index("row"), lax.axis_index("col")
    me = row * cols + col

    def place(index):
        return {"row": index // cols, "col": lax.rem(index, cols)}

    barrier = pltpu.get_barrier_semaphore()

    def greet(d, carry):
        pl.semaphore_signal(
            barrier, inc=1, device_id=place(lax.rem(me + d, GROUPS)), device_id_type=MESH
        )
        return carry

    lax.fori_loop(1, GROUPS, greet, 0)

    def exchange(phase, source, target):
        def copy(index, slot):
            return pltpu.make_async_remote_copy(
                src_ref=source.at[index],
                dst_ref=target.at[slot],
                send_sem=send_sem.at[phase, index],
                recv_sem=recv_sem.at[phase, slot],
                device_id=place(index),
                device_id_type=MESH,
            )

        def start(d, carry):
            copy(lax.rem(me + d, GROUPS), me).start()
            return carry

        def finish(d, carry):
            index = lax.rem(me + GROUPS - d, GROUPS)
            copy(index, index).wait_recv()
            return carry

        def drain(d, carry):
            copy(lax.rem(me + d, GROUPS), me).wait_send()
            return carry

        lax.fori_loop(1, GROUPS, start, 0)
        target[me] = source[me]
        lax.fori_loop(1, GROUPS, finish, 0)
        lax.fori_loop(1, GROUPS, drain, 0)

    sub = lax.broadcasted_iota(jnp.int32, (8, 128), 0)

    def spread_ids(ids):
        rows = []
        for t in range(SIDE // 8):
            v = jnp.full((8, 128), ids[8 * t], jnp.int32)
            for s in range(1, 8):
                v = jnp.where(sub == s, ids[8 * t + s], v)
            rows.append(v)
        return rows

    row_ids = [chain[row * SIDE + i] for i in range(SIDE)]
    col_ids = [chain[col * SIDE + i] for i in range(SIDE)]
    per_side = SIDE // MASK_TILE
    tiles = [
        [block_mask[row * per_side + a, col * per_side + b] for b in range(per_side)]
        for a in range(per_side)
    ]

    def mask_rows(update, i):
        lead, others = (row_ids, spread_cols) if update == 0 else (col_ids, spread_rows)
        parts = []
        for t in range(SIDE // 8):
            tile = tiles[i // 8][t] if update == 0 else tiles[t][i // 8]
            parts.append(
                jnp.where(others[t] == lead[i], 1, jnp.full((8, 128), tile, jnp.int32))
            )
        return jnp.concatenate(parts, axis=0).astype(jnp.float32)

    spread_rows, spread_cols = spread_ids(row_ids), spread_ids(col_ids)
    lane16 = lax.broadcasted_iota(jnp.int32, (16, 128), 1)
    lane8 = lax.broadcasted_iota(jnp.int32, (8, 128), 1)
    lane96 = lax.broadcasted_iota(jnp.int32, (4 * SIDE, 128), 1)
    edges[:, 72:80, :] = jnp.zeros((GROUPS, 8, 128), jnp.float32)
    same = (lax.broadcasted_iota(jnp.int32, (128, 768), 0) & 7) == (
        lax.broadcasted_iota(jnp.int32, (128, 768), 1) & 7
    )
    fold = jnp.where(
        lax.broadcasted_iota(jnp.int32, (16, 128), 1) // WIDTH
        == lax.broadcasted_iota(jnp.int32, (16, 128), 0),
        1.0,
        0.0,
    ).astype(jnp.bfloat16)

    for u in range(2):
        origin = pair if u == 0 else state
        for t in range(3):
            rows = pl.ds(192 * t, 192)
            normed = norm_rows(origin[rows, :], gain[2 * u : 2 * u + 1, :], bias[2 * u : 2 * u + 1, :])
            proj = jnp.dot(normed, w_proj[u], preferred_element_type=jnp.float32)
            left = sigmoid(proj[:, 0:128]) * proj[:, 128:256]
            right = sigmoid(proj[:, 256:384]) * proj[:, 384:512]
            gates[rows, :] = sigmoid(proj[:, 512:640])
            for s in range(8):
                mask = mask_rows(u, 8 * t + s)
                edges[s, pl.ds(24 * t, 24), :] = left[24 * s : 24 * s + 24] * mask
                edges[8 + s, pl.ds(24 * t, 24), :] = right[24 * s : 24 * s + 24] * mask
        for t in range(LR_ROWS // 16):
            rows = pl.ds(16 * t, 16)
            swapped = swap_groups([edges[a, rows, :] for a in range(GROUPS)], lane16)
            for g in range(GROUPS):
                lr_out[u, g, rows, :] = swapped[g].astype(jnp.bfloat16)

        if u == 0:
            pl.semaphore_wait(barrier, GROUPS - 1)
        exchange(2 * u, lr_out.at[u], lr_in.at[u])

        grid = {}
        for lead in range(4):
            slabs = []
            for k in range(4):
                index = lead * 4 + k if u == 0 else k * 4 + lead
                slabs.append(lr_in[u, index].astype(jnp.float32))
            for t in range(3):
                grid[lead, t] = jnp.concatenate(
                    [slab[24 * t : 24 * t + 24] for slab in slabs], axis=0
                )
        turned = {key: pltpu.roll(value, 64, 1) for key, value in grid.items()}
        low = lane96 < 64
        order = [(lead, t) for lead in range(4) for t in range(3)]
        rights = [jnp.where(low, turned[b, 0], grid[b, 1]) for b in range(4)]
        rights += [jnp.where(low, turned[b, 2], grid[b + 1, 2]) for b in (0, 2)]
        rights = jnp.concatenate([r.astype(jnp.bfloat16) for r in rights], axis=1)
        folded = []
        for q in range(6):
            lefts = jnp.where(low, grid[order[2 * q]], turned[order[2 * q + 1]])
            product = jnp.dot(
                lefts.T.astype(jnp.bfloat16), rights, preferred_element_type=jnp.float32
            )
            kept = jnp.where(same, product, 0.0).astype(jnp.bfloat16)
            folded.append(jnp.dot(fold, kept, preferred_element_type=jnp.float32))
        whole = jnp.concatenate(folded, axis=0)
        half = lane8 < 64
        for a in range(4):
            for b in range(4):
                block = whole[24 * a : 24 * a + 24]
                side = block[:, 512 + 128 * (b // 2) : 640 + 128 * (b // 2)]
                top, mid, end = side[0:8], side[8:16], side[16:24]
                if b % 2 == 0:
                    mixed = jnp.where(half, top, pltpu.roll(mid, 64, 1))
                else:
                    mixed = jnp.where(half, pltpu.roll(top, 64, 1), mid)
                    end = pltpu.roll(end, 64, 1)
                slab = jnp.concatenate(
                    [block[:, 128 * b : 128 * b + 128], mixed, end, jnp.zeros_like(end)], axis=0
                )
                tri_out[u, 4 * a + b] = slab.astype(jnp.bfloat16)

        exchange(2 * u + 1, tri_out.at[u], tri_in.at[u])

        for t in range(3):
            home = swap_groups(
                [
                    tri_in[u, g, pl.ds(16 * t, 16), :].astype(jnp.float32)
                    for g in range(GROUPS)
                ],
                lane16,
            )
            for a in range(GROUPS):
                if t == 0:
                    tri[pl.ds(24 * a, 16), :] = home[a]
                elif t == 1:
                    tri[pl.ds(24 * a + 16, 8), :] = home[a][0:8]
                    tri[pl.ds(24 * (16 + a % 8) + 8 * (a // 8), 8), :] = home[a][8:16]
                elif a < 8:
                    tri[pl.ds(24 * (16 + a) + 16, 8), :] = home[a][0:8]

        for t in range(3):
            rows = pl.ds(192 * t, 192)
            tri_norm = norm_rows(
                tri[rows, :], gain[2 * u + 1 : 2 * u + 2, :], bias[2 * u + 1 : 2 * u + 2, :]
            )
            change = jnp.dot(tri_norm, w_out[u], preferred_element_type=jnp.float32)
            if u == 0:
                for s in range(8):
                    across = pl.ds(8 * t + s, SIDE, stride=SIDE)
                    state[pl.ds(192 * t + 24 * s, 24), :] = (
                        pair[across, :] + gates[across, :] * change[24 * s : 24 * s + 24]
                    )
            else:
                state[rows, :] = state[rows, :] + gates[rows, :] * change

    hidden = w_down.shape[0]
    for t in range(3):
        rows = pl.ds(192 * t, 192)
        values = state[rows, :]
        normed = norm_rows(values, gain[4:5, :], bias[4:5, :])
        pre = jnp.dot(normed, w_in[...], preferred_element_type=jnp.float32)
        gate = pre[:, :hidden]
        act = (gate * sigmoid(gate) * pre[:, hidden:]).astype(jnp.bfloat16)
        out[rows, :] = values + jnp.dot(act, w_down[...], preferred_element_type=jnp.float32)


def split_channels(cols, pair, chain, block_mask, gain, bias, w_proj, w_out, w_in, w_down):
    rows = pair.shape[0] * pair.shape[1]
    vmem, smem = pl.BlockSpec(memory_space=pltpu.VMEM), pl.BlockSpec(memory_space=pltpu.SMEM)
    result = pl.pallas_call(
        functools.partial(kernel, cols),
        out_shape=jax.ShapeDtypeStruct((rows, 128), jnp.float32),
        in_specs=[vmem, smem, smem] + [vmem] * 6,
        out_specs=vmem,
        scratch_shapes=[
            pltpu.VMEM((GROUPS, LR_ROWS, 128), jnp.float32),
            pltpu.VMEM((rows, 128), jnp.float32),
            pltpu.VMEM((rows, 128), jnp.float32),
            pltpu.VMEM((rows, 128), jnp.float32),
            pltpu.VMEM((2, GROUPS, LR_ROWS, 128), jnp.bfloat16),
            pltpu.VMEM((2, GROUPS, LR_ROWS, 128), jnp.bfloat16),
            pltpu.VMEM((2, GROUPS, TRI_ROWS, 128), jnp.bfloat16),
            pltpu.VMEM((2, GROUPS, TRI_ROWS, 128), jnp.bfloat16),
            pltpu.SemaphoreType.DMA((4, GROUPS)),
            pltpu.SemaphoreType.DMA((4, GROUPS)),
        ],
        compiler_params=pltpu.CompilerParams(
            collective_id=0, has_side_effects=True, vmem_limit_bytes=40 * 1024 * 1024
        ),
        cost_estimate=pl.CostEstimate(
            flops=900_000_000, bytes_accessed=2_000_000, transcendentals=1_000_000
        ),
    )(pair.reshape(rows, 128), chain, block_mask, gain, bias, w_proj, w_out, w_in, w_down)
    return result.reshape(pair.shape[1], pair.shape[0], 128).swapaxes(0, 1)


def solution(mesh):
    if mesh.shape["row"] == 4 and mesh.shape["col"] == 4:
        body = functools.partial(split_channels, mesh.shape["col"])
    else:
        body = local
    return jax.shard_map(
        body,
        mesh=mesh,
        in_specs=(
            P(("parts", "row"), "col", None),
            P("parts"),
            P("parts", None),
            P(),
            P(),
            P(),
            P(),
            P(),
            P(),
        ),
        out_specs=P(("parts", "row"), "col", None),
        check_vma=False,
    )
```

```python
import functools

import jax
import jax.numpy as jnp
from jax import lax
from jax.experimental import pallas as pl
from jax.experimental.pallas import tpu as pltpu
from jax.sharding import PartitionSpec as P

MASK_TILE = 8
MESH = pl.DeviceIdType.MESH


def broadcast(array, axis, root):
    mine = lax.axis_index(axis) == root
    return lax.psum(jnp.where(mine, array, jnp.zeros_like(array)), axis)


def layer_norm(values, gain, bias):
    center = jnp.mean(values, axis=-1, keepdims=True)
    spread = jnp.mean((values - center) ** 2, axis=-1, keepdims=True)
    return (values - center) * lax.rsqrt(spread + 1e-05) * gain + bias


def project_edges(state, pair_mask, norm_gain, norm_bias, w_proj, update):
    channels = state.shape[2]
    normed = layer_norm(state, norm_gain[2 * update], norm_bias[2 * update]).astype(jnp.bfloat16)
    proj = jnp.dot(normed, w_proj[update], preferred_element_type=jnp.float32)
    left_edge = (
        jax.nn.sigmoid(proj[..., 0:channels]) * proj[..., channels : 2 * channels] * pair_mask
    ).astype(jnp.bfloat16)
    right_edge = (
        jax.nn.sigmoid(proj[..., 2 * channels : 3 * channels])
        * proj[..., 3 * channels : 4 * channels]
        * pair_mask
    ).astype(jnp.bfloat16)
    gating = jax.nn.sigmoid(proj[..., 4 * channels :])
    return (left_edge, right_edge, gating)


def finish_update(state, triangle, gating, norm_gain, norm_bias, w_out, update):
    tri_norm = layer_norm(triangle, norm_gain[2 * update + 1], norm_bias[2 * update + 1]).astype(
        jnp.bfloat16
    )
    return state + gating * jnp.dot(tri_norm, w_out[update], preferred_element_type=jnp.float32)


def local(pair, chain, block_mask, norm_gain, norm_bias, w_proj, w_out, w_trans_in, w_trans_out):
    extent = pair.shape[0]
    row_offset = lax.axis_index("row") * extent
    col_offset = lax.axis_index("col") * extent
    row_chain = lax.dynamic_slice_in_dim(chain, row_offset, extent)
    col_chain = lax.dynamic_slice_in_dim(chain, col_offset, extent)
    expanded = jnp.repeat(jnp.repeat(block_mask, MASK_TILE, axis=0), MASK_TILE, axis=1)
    local_blocks = lax.dynamic_slice(expanded, (row_offset, col_offset), (extent, extent)) > 0
    same_chain = row_chain[:, None] == col_chain[None, :]
    pair_mask = jnp.logical_or(same_chain, local_blocks).astype(jnp.float32)[..., None]
    state = pair
    left_edge, right_edge, gating = project_edges(state, pair_mask, norm_gain, norm_bias, w_proj, 0)
    right_strip = lax.all_gather(right_edge, "col", axis=1, tiled=True)
    mirrored_right = broadcast(right_strip, "row", lax.axis_index("col"))
    partner = mirrored_right
    triangle = jnp.einsum(
        "ikc,jkc->ijc",
        lax.all_gather(left_edge, "col", axis=1, tiled=True),
        partner,
        preferred_element_type=jnp.float32,
    )
    state = finish_update(state, triangle, gating, norm_gain, norm_bias, w_out, 0)
    left_edge, right_edge, gating = project_edges(state, pair_mask, norm_gain, norm_bias, w_proj, 1)
    left_strip = lax.all_gather(left_edge, "row", axis=0, tiled=True)
    mirrored_left = broadcast(left_strip, "col", lax.axis_index("row"))
    partner = mirrored_left
    triangle = jnp.einsum(
        "kic,kjc->ijc",
        partner,
        lax.all_gather(right_edge, "row", axis=0, tiled=True),
        preferred_element_type=jnp.float32,
    )
    state = finish_update(state, triangle, gating, norm_gain, norm_bias, w_out, 1)
    trans_norm = layer_norm(state, norm_gain[4], norm_bias[4]).astype(jnp.bfloat16)
    hidden_pre = jnp.dot(trans_norm, w_trans_in, preferred_element_type=jnp.float32)
    width = w_trans_out.shape[0]
    activated = (jax.nn.silu(hidden_pre[..., :width]) * hidden_pre[..., width:]).astype(
        jnp.bfloat16
    )
    return state + jnp.dot(activated, w_trans_out, preferred_element_type=jnp.float32)


GROUPS = 16
WIDTH = 8
SIDE = 24
LR_ROWS = 80
HEAD_ROWS = 48
TRI_ROWS = 48


def sigmoid(x):
    return 0.5 * jnp.tanh(0.5 * x) + 0.5


def swap_groups(values, lane):
    values = list(values)
    for step in (8, 4, 2, 1):
        low = (lane & (step * WIDTH)) == 0
        for a in range(GROUPS):
            if a & step:
                continue
            first, second = values[a], values[a + step]
            values[a] = jnp.where(low, first, pltpu.roll(second, step * WIDTH, 1))
            values[a + step] = jnp.where(low, pltpu.roll(first, 128 - step * WIDTH, 1), second)
    return values


def norm_rows(x, gain, bias):
    center = jnp.mean(x, axis=-1, keepdims=True)
    off = x - center
    spread = jnp.mean(off * off, axis=-1, keepdims=True)
    return (off * lax.rsqrt(spread + 1e-05) * gain + bias).astype(jnp.bfloat16)


def kernel(
    cols, pair_hbm, chain_hbm, block_hbm, gain_hbm, bias_hbm, proj_hbm, out_hbm, in_hbm, down_hbm,
    out, pair, chain, block_mask, gain, bias, w_proj, w_out, w_in, w_down,
    edges, normed, gates, state, tri, grid, lr_out, lr_in, tri_out, tri_in,
    load_sem, send_sem, recv_sem,
):
    row, col = lax.axis_index("row"), lax.axis_index("col")
    me = row * cols + col
    loads = [
        pltpu.make_async_copy(src, dst, load_sem.at[n])
        for n, (src, dst) in enumerate(
            (
                (pair_hbm, pair),
                (chain_hbm, chain),
                (block_hbm, block_mask),
                (gain_hbm, gain),
                (bias_hbm, bias),
                (proj_hbm, w_proj),
                (out_hbm, w_out),
                (in_hbm, w_in),
                (down_hbm, w_down),
            )
        )
    ]
    for load in loads:
        load.start()

    def place(index):
        return {"row": index // cols, "col": lax.rem(index, cols)}

    barrier = pltpu.get_barrier_semaphore()

    def greet(d, carry):
        pl.semaphore_signal(
            barrier, inc=1, device_id=place(lax.rem(me + d, GROUPS)), device_id_type=MESH
        )
        return carry

    lax.fori_loop(1, GROUPS, greet, 0)

    def remote(phase, source, target, index, slot):
        return pltpu.make_async_remote_copy(
            src_ref=source.at[index],
            dst_ref=target.at[slot],
            send_sem=send_sem.at[phase, index],
            recv_sem=recv_sem.at[phase, slot],
            device_id=place(index),
            device_id_type=MESH,
        )

    def edge_copy(u, piece, index, slot):
        start, count = ((0, HEAD_ROWS), (HEAD_ROWS, LR_ROWS - HEAD_ROWS))[piece]
        return pltpu.make_async_remote_copy(
            src_ref=lr_out.at[u, index, pl.ds(start, count)],
            dst_ref=lr_in.at[u, slot, pl.ds(start, count)],
            send_sem=send_sem.at[3 * u + piece, index],
            recv_sem=recv_sem.at[3 * u + piece, slot],
            device_id=place(index),
            device_id_type=MESH,
        )

    def tri_copy(u, index, slot):
        return remote(3 * u + 2, tri_out.at[u], tri_in.at[u], index, slot)

    def each_peer(action):
        def body(d, carry):
            action(lax.rem(me + d, GROUPS))
            return carry

        lax.fori_loop(1, GROUPS, body, 0)

    sub = lax.broadcasted_iota(jnp.int32, (8, 128), 0)

    def spread_ids(ids):
        rows = []
        for t in range(SIDE // 8):
            v = jnp.full((8, 128), ids[8 * t], jnp.int32)
            for s in range(1, 8):
                v = jnp.where(sub == s, ids[8 * t + s], v)
            rows.append(v)
        return rows

    for n in range(5):
        loads[n].wait()
    row_ids = [chain[row * SIDE + i] for i in range(SIDE)]
    col_ids = [chain[col * SIDE + i] for i in range(SIDE)]
    per_side = SIDE // MASK_TILE
    tiles = [
        [block_mask[row * per_side + a, col * per_side + b] for b in range(per_side)]
        for a in range(per_side)
    ]

    def mask_tile(update, i, t):
        lead, others = (row_ids, spread_cols) if update == 0 else (col_ids, spread_rows)
        tile = tiles[i // 8][t] if update == 0 else tiles[t][i // 8]
        return jnp.where(
            others[t] == lead[i], 1, jnp.full((8, 128), tile, jnp.int32)
        ).astype(jnp.float32)

    spread_rows, spread_cols = spread_ids(row_ids), spread_ids(col_ids)
    lane16 = lax.broadcasted_iota(jnp.int32, (16, 128), 1)
    lane8 = lax.broadcasted_iota(jnp.int32, (8, 128), 1)
    low96 = lax.broadcasted_iota(jnp.int32, (4 * SIDE, 128), 1) < 64
    edges[:, 72:80, :] = jnp.zeros((GROUPS, 8, 128), jnp.float32)
    same = (lax.broadcasted_iota(jnp.int32, (128, 768), 0) & 7) == (
        lax.broadcasted_iota(jnp.int32, (128, 768), 1) & 7
    )
    fold = jnp.where(
        lax.broadcasted_iota(jnp.int32, (16, 128), 1) // WIDTH
        == lax.broadcasted_iota(jnp.int32, (16, 128), 0),
        1.0,
        0.0,
    ).astype(jnp.bfloat16)
    loads[5].wait()

    for u in range(2):
        origin = pair if u == 0 else state
        for chunk in range(3):
            piece = chunk // 2
            first, lines, depth = ((0, 12, 16), (12, 12, 16), (0, 24, 8))[chunk]
            base = 16 * piece
            values = jnp.concatenate(
                [origin[pl.ds(24 * (first + n) + base, depth), :] for n in range(lines)], axis=0
            )
            unit = norm_rows(values, gain[2 * u : 2 * u + 1, :], bias[2 * u : 2 * u + 1, :])
            normed[pl.ds(192 * chunk, 192), :] = unit
            proj = jnp.dot(unit, w_proj[u, :, 0:512], preferred_element_type=jnp.float32)
            left = sigmoid(proj[:, 0:128]) * proj[:, 128:256]
            right = sigmoid(proj[:, 256:384]) * proj[:, 384:512]
            for n in range(lines):
                i = first + n
                for h in range(depth // 8):
                    mask = mask_tile(u, i, base // 8 + h)
                    rows = pl.ds(48 * piece + depth * (i // 8) + 8 * h, 8)
                    at = n * depth + 8 * h
                    edges[i % 8, rows, :] = left[at : at + 8] * mask
                    edges[8 + i % 8, rows, :] = right[at : at + 8] * mask
            if chunk == 0:
                continue
            for t in ((0, 1, 2), (3, 4))[piece]:
                rows = pl.ds(16 * t, 16)
                swapped = swap_groups([edges[a, rows, :] for a in range(GROUPS)], lane16)
                for g in range(GROUPS):
                    lr_out[u, g, rows, :] = swapped[g].astype(jnp.bfloat16)
            if u == 0 and piece == 0:
                pl.semaphore_wait(barrier, GROUPS - 1)
            each_peer(lambda index: edge_copy(u, piece, index, me).start())

        for chunk in range(3):
            first, lines, depth = ((0, 12, 16), (12, 12, 16), (0, 24, 8))[chunk]
            gate = sigmoid(
                jnp.dot(
                    normed[pl.ds(192 * chunk, 192), :],
                    w_proj[u, :, 512:640],
                    preferred_element_type=jnp.float32,
                )
            )
            for n in range(lines):
                gates[pl.ds(24 * (first + n) + 16 * (chunk // 2), depth), :] = gate[
                    depth * n : depth * n + depth
                ]

        def unpack(source, index):
            if u == 0:
                lead, k = index // 4, lax.rem(index, 4)
            else:
                lead, k = lax.rem(index, 4), index // 4
            at = pl.multiple_of(24 * k, 8)
            slab = source[u, index].astype(jnp.float32)
            for t in range(3):
                grid[3 * lead + t, pl.ds(at, 16), :] = slab[16 * t : 16 * t + 16]
                grid[3 * lead + t, pl.ds(at + 16, 8), :] = slab[48 + 8 * t : 56 + 8 * t]

        unpack(lr_out, me)

        def take(d, carry):
            index = lax.rem(me + GROUPS - d, GROUPS)
            edge_copy(u, 0, index, index).wait_recv()
            edge_copy(u, 1, index, index).wait_recv()
            unpack(lr_in, index)
            return carry

        lax.fori_loop(1, GROUPS, take, 0)

        rights = [
            jnp.where(low96, pltpu.roll(grid[3 * b], 64, 1), grid[3 * b + 1]) for b in range(4)
        ]
        rights += [
            jnp.where(low96, pltpu.roll(grid[3 * b + 2], 64, 1), grid[3 * b + 5]) for b in (0, 2)
        ]
        rights = jnp.concatenate([r.astype(jnp.bfloat16) for r in rights], axis=1)
        half = lane8 < 64
        for step in (2, 1, 3, 0):
            lead = lax.rem(row + step, 4)
            pairs = jnp.where(low96, grid[3 * lead], pltpu.roll(grid[3 * lead + 1], 64, 1))
            product = jnp.dot(
                pairs.T.astype(jnp.bfloat16), rights, preferred_element_type=jnp.float32
            )
            kept = jnp.where(same, product, 0.0).astype(jnp.bfloat16)
            upper = jnp.dot(fold, kept, preferred_element_type=jnp.float32)
            product = jnp.dot(
                grid[3 * lead + 2].T[0:64].astype(jnp.bfloat16),
                rights,
                preferred_element_type=jnp.float32,
            )
            kept = jnp.where(same[0:64], product, 0.0).astype(jnp.bfloat16)
            lower = jnp.dot(fold[0:8, 0:64], kept, preferred_element_type=jnp.float32)
            for b in range(4):
                spot = 512 + 128 * (b // 2)
                top, mid = upper[0:8, spot : spot + 128], upper[8:16, spot : spot + 128]
                end = lower[:, spot : spot + 128]
                if b % 2 == 0:
                    mixed = jnp.where(half, top, pltpu.roll(mid, 64, 1))
                else:
                    mixed = jnp.where(half, pltpu.roll(top, 64, 1), mid)
                    end = pltpu.roll(end, 64, 1)
                lanes = slice(128 * b, 128 * b + 128)
                slab = jnp.concatenate(
                    [upper[:, lanes], lower[:, lanes], mixed, end, jnp.zeros_like(end)], axis=0
                )
                tri_out[u, 4 * lead + b] = slab.astype(jnp.bfloat16)
            for b in range(0 if step else 1, 4):
                tri_copy(u, 4 * lead + lax.rem(col + b, 4), me).start()
        tri_in[u, me] = tri_out[u, me]
        each_peer(lambda index: tri_copy(u, index, index).wait_recv())
        if u == 0:
            for n in range(6, 9):
                loads[n].wait()

        for t in range(3):
            home = swap_groups(
                [
                    tri_in[u, g, pl.ds(16 * t, 16), :].astype(jnp.float32)
                    for g in range(GROUPS)
                ],
                lane16,
            )
            for a in range(GROUPS):
                if t == 0:
                    tri[pl.ds(24 * a, 16), :] = home[a]
                elif t == 1:
                    tri[pl.ds(24 * a + 16, 8), :] = home[a][0:8]
                    tri[pl.ds(24 * (16 + a % 8) + 8 * (a // 8), 8), :] = home[a][8:16]
                elif a < 8:
                    tri[pl.ds(24 * (16 + a) + 16, 8), :] = home[a][0:8]

        for t in range(3):
            rows = pl.ds(192 * t, 192)
            tri_norm = norm_rows(
                tri[rows, :], gain[2 * u + 1 : 2 * u + 2, :], bias[2 * u + 1 : 2 * u + 2, :]
            )
            change = jnp.dot(tri_norm, w_out[u], preferred_element_type=jnp.float32)
            if u == 0:
                for s in range(8):
                    across = pl.ds(8 * t + s, SIDE, stride=SIDE)
                    state[pl.ds(192 * t + 24 * s, 24), :] = (
                        pair[across, :] + gates[across, :] * change[24 * s : 24 * s + 24]
                    )
            else:
                state[rows, :] = state[rows, :] + gates[rows, :] * change

    hidden = w_down.shape[0]
    for t in range(3):
        rows = pl.ds(192 * t, 192)
        values = state[rows, :]
        unit = norm_rows(values, gain[4:5, :], bias[4:5, :])
        pre = jnp.dot(unit, w_in[...], preferred_element_type=jnp.float32)
        gate = pre[:, :hidden]
        act = (gate * sigmoid(gate) * pre[:, hidden:]).astype(jnp.bfloat16)
        out[rows, :] = values + jnp.dot(act, w_down[...], preferred_element_type=jnp.float32)
    for u in range(2):
        for piece in range(2):
            each_peer(lambda index: edge_copy(u, piece, index, me).wait_send())
        each_peer(lambda index: tri_copy(u, index, me).wait_send())


def split_channels(cols, pair, chain, block_mask, gain, bias, w_proj, w_out, w_in, w_down):
    rows = pair.shape[0] * pair.shape[1]
    vmem, hbm = pl.BlockSpec(memory_space=pltpu.VMEM), pl.BlockSpec(memory_space=pltpu.HBM)
    operands = (
        pair.reshape(rows, 128), chain, block_mask, gain, bias, w_proj, w_out, w_in, w_down
    )
    result = pl.pallas_call(
        functools.partial(kernel, cols),
        out_shape=jax.ShapeDtypeStruct((rows, 128), jnp.float32),
        in_specs=[hbm] * 9,
        out_specs=vmem,
        scratch_shapes=[
            (pltpu.SMEM if n in (1, 2) else pltpu.VMEM)(array.shape, array.dtype)
            for n, array in enumerate(operands)
        ]
        + [
            pltpu.VMEM((GROUPS, LR_ROWS, 128), jnp.float32),
            pltpu.VMEM((rows, 128), jnp.bfloat16),
            pltpu.VMEM((rows, 128), jnp.float32),
            pltpu.VMEM((rows, 128), jnp.float32),
            pltpu.VMEM((rows, 128), jnp.float32),
            pltpu.VMEM((12, 4 * SIDE, 128), jnp.float32),
            pltpu.VMEM((2, GROUPS, LR_ROWS, 128), jnp.bfloat16),
            pltpu.VMEM((2, GROUPS, LR_ROWS, 128), jnp.bfloat16),
            pltpu.VMEM((2, GROUPS, TRI_ROWS, 128), jnp.bfloat16),
            pltpu.VMEM((2, GROUPS, TRI_ROWS, 128), jnp.bfloat16),
            pltpu.SemaphoreType.DMA((9,)),
            pltpu.SemaphoreType.DMA((6, GROUPS)),
            pltpu.SemaphoreType.DMA((6, GROUPS)),
        ],
        compiler_params=pltpu.CompilerParams(
            collective_id=0, has_side_effects=True, vmem_limit_bytes=40 * 1024 * 1024
        ),
        cost_estimate=pl.CostEstimate(
            flops=900_000_000, bytes_accessed=2_000_000, transcendentals=1_000_000
        ),
    )(*operands)
    return result.reshape(pair.shape[1], pair.shape[0], 128).swapaxes(0, 1)


def solution(mesh):
    if mesh.shape["row"] == 4 and mesh.shape["col"] == 4:
        body = functools.partial(split_channels, mesh.shape["col"])
    else:
        body = local
    return jax.shard_map(
        body,
        mesh=mesh,
        in_specs=(
            P(("parts", "row"), "col", None),
            P("parts"),
            P("parts", None),
            P(),
            P(),
            P(),
            P(),
            P(),
            P(),
        ),
        out_specs=P(("parts", "row"), "col", None),
        check_vma=False,
    )
```

```python
import functools

import jax
import jax.numpy as jnp
from jax import lax
from jax.experimental import pallas as pl
from jax.experimental.pallas import tpu as pltpu
from jax.sharding import PartitionSpec as P

MASK_TILE = 8
MESH = pl.DeviceIdType.MESH


def broadcast(array, axis, root):
    mine = lax.axis_index(axis) == root
    return lax.psum(jnp.where(mine, array, jnp.zeros_like(array)), axis)


def layer_norm(values, gain, bias):
    center = jnp.mean(values, axis=-1, keepdims=True)
    spread = jnp.mean((values - center) ** 2, axis=-1, keepdims=True)
    return (values - center) * lax.rsqrt(spread + 1e-05) * gain + bias


def project_edges(state, pair_mask, norm_gain, norm_bias, w_proj, update):
    channels = state.shape[2]
    normed = layer_norm(state, norm_gain[2 * update], norm_bias[2 * update]).astype(jnp.bfloat16)
    proj = jnp.dot(normed, w_proj[update], preferred_element_type=jnp.float32)
    left_edge = (
        jax.nn.sigmoid(proj[..., 0:channels]) * proj[..., channels : 2 * channels] * pair_mask
    ).astype(jnp.bfloat16)
    right_edge = (
        jax.nn.sigmoid(proj[..., 2 * channels : 3 * channels])
        * proj[..., 3 * channels : 4 * channels]
        * pair_mask
    ).astype(jnp.bfloat16)
    gating = jax.nn.sigmoid(proj[..., 4 * channels :])
    return (left_edge, right_edge, gating)


def finish_update(state, triangle, gating, norm_gain, norm_bias, w_out, update):
    tri_norm = layer_norm(triangle, norm_gain[2 * update + 1], norm_bias[2 * update + 1]).astype(
        jnp.bfloat16
    )
    return state + gating * jnp.dot(tri_norm, w_out[update], preferred_element_type=jnp.float32)


def local(pair, chain, block_mask, norm_gain, norm_bias, w_proj, w_out, w_trans_in, w_trans_out):
    extent = pair.shape[0]
    row_offset = lax.axis_index("row") * extent
    col_offset = lax.axis_index("col") * extent
    row_chain = lax.dynamic_slice_in_dim(chain, row_offset, extent)
    col_chain = lax.dynamic_slice_in_dim(chain, col_offset, extent)
    expanded = jnp.repeat(jnp.repeat(block_mask, MASK_TILE, axis=0), MASK_TILE, axis=1)
    local_blocks = lax.dynamic_slice(expanded, (row_offset, col_offset), (extent, extent)) > 0
    same_chain = row_chain[:, None] == col_chain[None, :]
    pair_mask = jnp.logical_or(same_chain, local_blocks).astype(jnp.float32)[..., None]
    state = pair
    left_edge, right_edge, gating = project_edges(state, pair_mask, norm_gain, norm_bias, w_proj, 0)
    right_strip = lax.all_gather(right_edge, "col", axis=1, tiled=True)
    mirrored_right = broadcast(right_strip, "row", lax.axis_index("col"))
    partner = mirrored_right
    triangle = jnp.einsum(
        "ikc,jkc->ijc",
        lax.all_gather(left_edge, "col", axis=1, tiled=True),
        partner,
        preferred_element_type=jnp.float32,
    )
    state = finish_update(state, triangle, gating, norm_gain, norm_bias, w_out, 0)
    left_edge, right_edge, gating = project_edges(state, pair_mask, norm_gain, norm_bias, w_proj, 1)
    left_strip = lax.all_gather(left_edge, "row", axis=0, tiled=True)
    mirrored_left = broadcast(left_strip, "col", lax.axis_index("row"))
    partner = mirrored_left
    triangle = jnp.einsum(
        "kic,kjc->ijc",
        partner,
        lax.all_gather(right_edge, "row", axis=0, tiled=True),
        preferred_element_type=jnp.float32,
    )
    state = finish_update(state, triangle, gating, norm_gain, norm_bias, w_out, 1)
    trans_norm = layer_norm(state, norm_gain[4], norm_bias[4]).astype(jnp.bfloat16)
    hidden_pre = jnp.dot(trans_norm, w_trans_in, preferred_element_type=jnp.float32)
    width = w_trans_out.shape[0]
    activated = (jax.nn.silu(hidden_pre[..., :width]) * hidden_pre[..., width:]).astype(
        jnp.bfloat16
    )
    return state + jnp.dot(activated, w_trans_out, preferred_element_type=jnp.float32)


GROUPS = 16
WIDTH = 8
SIDE = 24
LR_TILES = 9
TRI_TILES = 5


def sigmoid(x):
    return 0.5 * jnp.tanh(0.5 * x) + 0.5


def swap_groups(values, lane):
    values = list(values)
    for step in (8, 4, 2, 1):
        low = (lane & (step * WIDTH)) == 0
        for a in range(GROUPS):
            if a & step:
                continue
            first, second = values[a], values[a + step]
            values[a] = jnp.where(low, first, pltpu.roll(second, step * WIDTH, 1))
            values[a + step] = jnp.where(low, pltpu.roll(first, 128 - step * WIDTH, 1), second)
    return values


def norm_rows(x, gain, bias):
    center = jnp.mean(x, axis=-1, keepdims=True)
    off = x - center
    spread = jnp.mean(off * off, axis=-1, keepdims=True)
    return (off * lax.rsqrt(spread + 1e-05) * gain + bias).astype(jnp.bfloat16)


def kernel(
    cols, pair_hbm, chain_hbm, block_hbm, gain_hbm, bias_hbm, proj_hbm, out_hbm, in_hbm, down_hbm,
    out, pair, chain, block_mask, gain, bias, w_proj, w_out, w_in, w_down,
    edges, normed, gates, state, tri, grid, lr_out, lr_in, tri_out, tri_in,
    load_sem, send_sem, recv_sem,
):
    row, col = lax.axis_index("row"), lax.axis_index("col")
    me = row * cols + col
    loads = [
        pltpu.make_async_copy(src, dst, load_sem.at[n])
        for n, (src, dst) in enumerate(
            (
                (pair_hbm, pair),
                (chain_hbm, chain),
                (block_hbm, block_mask),
                (gain_hbm, gain),
                (bias_hbm, bias),
                (proj_hbm, w_proj),
                (out_hbm, w_out),
                (in_hbm, w_in),
                (down_hbm, w_down),
            )
        )
    ]
    for load in loads:
        load.start()

    def place(index):
        return {"row": index // cols, "col": lax.rem(index, cols)}

    barrier = pltpu.get_barrier_semaphore()

    def greet(d, carry):
        pl.semaphore_signal(
            barrier, inc=1, device_id=place(lax.rem(me + d, GROUPS)), device_id_type=MESH
        )
        return carry

    lax.fori_loop(1, GROUPS, greet, 0)

    def remote(phase, source, target, index, slot):
        return pltpu.make_async_remote_copy(
            src_ref=source.at[index],
            dst_ref=target.at[slot],
            send_sem=send_sem.at[phase, index],
            recv_sem=recv_sem.at[phase, slot],
            device_id=place(index),
            device_id_type=MESH,
        )

    def edge_copy(u, index, slot):
        return remote(2 * u, lr_out.at[u], lr_in.at[u], index, slot)

    def tri_copy(u, index, slot):
        return remote(2 * u + 1, tri_out.at[u], tri_in.at[u], index, slot)

    def each_peer(action):
        def body(d, carry):
            action(lax.rem(me + d, GROUPS))
            return carry

        lax.fori_loop(1, GROUPS, body, 0)

    sub = lax.broadcasted_iota(jnp.int32, (8, 128), 0)

    def spread_ids(ids):
        rows = []
        for t in range(SIDE // 8):
            v = jnp.full((8, 128), ids[8 * t], jnp.int32)
            for s in range(1, 8):
                v = jnp.where(sub == s, ids[8 * t + s], v)
            rows.append(v)
        return rows

    for n in range(5):
        loads[n].wait()
    row_ids = [chain[row * SIDE + i] for i in range(SIDE)]
    col_ids = [chain[col * SIDE + i] for i in range(SIDE)]
    per_side = SIDE // MASK_TILE
    tiles = [
        [block_mask[row * per_side + a, col * per_side + b] for b in range(per_side)]
        for a in range(per_side)
    ]

    def mask_tile(update, i, t):
        lead, others = (row_ids, spread_cols) if update == 0 else (col_ids, spread_rows)
        tile = tiles[i // 8][t] if update == 0 else tiles[t][i // 8]
        return jnp.where(
            others[t] == lead[i], 1, jnp.full((8, 128), tile, jnp.int32)
        ).astype(jnp.float32)

    spread_rows, spread_cols = spread_ids(row_ids), spread_ids(col_ids)
    lane8 = lax.broadcasted_iota(jnp.int32, (8, 128), 1)
    low96 = lax.broadcasted_iota(jnp.int32, (4 * SIDE, 128), 1) < 64
    same = (lax.broadcasted_iota(jnp.int32, (128, 768), 0) & 7) == (
        lax.broadcasted_iota(jnp.int32, (128, 768), 1) & 7
    )
    fold = jnp.where(
        lax.broadcasted_iota(jnp.int32, (16, 128), 1) // WIDTH
        == lax.broadcasted_iota(jnp.int32, (16, 128), 0),
        1.0,
        0.0,
    ).astype(jnp.bfloat16)
    loads[5].wait()

    for u in range(2):
        origin = pair if u == 0 else state
        for chunk in range(3):
            piece = chunk // 2
            first, lines, depth = ((0, 12, 16), (12, 12, 16), (0, 24, 8))[chunk]
            base = 16 * piece
            values = jnp.concatenate(
                [origin[pl.ds(24 * (first + n) + base, depth), :] for n in range(lines)], axis=0
            )
            unit = norm_rows(values, gain[2 * u : 2 * u + 1, :], bias[2 * u : 2 * u + 1, :])
            normed[pl.ds(192 * chunk, 192), :] = unit
            proj = jnp.dot(unit, w_proj[u, :, 0:512], preferred_element_type=jnp.float32)
            left = sigmoid(proj[:, 0:128]) * proj[:, 128:256]
            right = sigmoid(proj[:, 256:384]) * proj[:, 384:512]
            for n in range(lines):
                i = first + n
                for h in range(depth // 8):
                    mask = mask_tile(u, i, base // 8 + h)
                    rows = pl.ds(48 * piece + depth * (i // 8) + 8 * h, 8)
                    at = n * depth + 8 * h
                    edges[i % 8, rows, :] = left[at : at + 8] * mask
                    edges[8 + i % 8, rows, :] = right[at : at + 8] * mask
            for t in ((), range(6), range(6, LR_TILES))[chunk]:
                rows = pl.ds(8 * t, 8)
                swapped = swap_groups([edges[a, rows, :] for a in range(GROUPS)], lane8)
                for g in range(GROUPS):
                    lr_out[u, g, t] = swapped[g].astype(jnp.bfloat16)
        if u == 0:
            pl.semaphore_wait(barrier, GROUPS - 1)
        each_peer(lambda index: edge_copy(u, index, me).start())

        for chunk in range(3):
            first, lines, depth = ((0, 12, 16), (12, 12, 16), (0, 24, 8))[chunk]
            gate = sigmoid(
                jnp.dot(
                    normed[pl.ds(192 * chunk, 192), :],
                    w_proj[u, :, 512:640],
                    preferred_element_type=jnp.float32,
                )
            )
            for n in range(lines):
                gates[pl.ds(24 * (first + n) + 16 * (chunk // 2), depth), :] = gate[
                    depth * n : depth * n + depth
                ]

        def unpack(source, index):
            if u == 0:
                lead, k = index // 4, lax.rem(index, 4)
            else:
                lead, k = lax.rem(index, 4), index // 4
            at = pl.multiple_of(24 * k, 8)
            slab = source[u, index].astype(jnp.float32).reshape(8 * LR_TILES, 128)
            for t in range(3):
                grid[3 * lead + t, pl.ds(at, 16), :] = slab[16 * t : 16 * t + 16]
                grid[3 * lead + t, pl.ds(at + 16, 8), :] = slab[48 + 8 * t : 56 + 8 * t]

        unpack(lr_out, me)

        def take(d, carry):
            index = lax.rem(me + GROUPS - d, GROUPS)
            edge_copy(u, index, index).wait_recv()
            unpack(lr_in, index)
            return carry

        lax.fori_loop(1, GROUPS, take, 0)

        rights = [
            jnp.where(low96, pltpu.roll(grid[3 * b], 64, 1), grid[3 * b + 1]) for b in range(4)
        ]
        rights += [
            jnp.where(low96, pltpu.roll(grid[3 * b + 2], 64, 1), grid[3 * b + 5]) for b in (0, 2)
        ]
        rights = jnp.concatenate([r.astype(jnp.bfloat16) for r in rights], axis=1)
        half = lane8 < 64
        for step in (2, 1, 3, 0):
            lead = lax.rem(row + step, 4)
            pairs = jnp.where(low96, grid[3 * lead], pltpu.roll(grid[3 * lead + 1], 64, 1))
            product = jnp.dot(
                pairs.T.astype(jnp.bfloat16), rights, preferred_element_type=jnp.float32
            )
            kept = jnp.where(same, product, 0.0).astype(jnp.bfloat16)
            upper = jnp.dot(fold, kept, preferred_element_type=jnp.float32)
            product = jnp.dot(
                grid[3 * lead + 2].T[0:64].astype(jnp.bfloat16),
                rights,
                preferred_element_type=jnp.float32,
            )
            kept = jnp.where(same[0:64], product, 0.0).astype(jnp.bfloat16)
            lower = jnp.dot(fold[0:8, 0:64], kept, preferred_element_type=jnp.float32)
            for b in range(4):
                spot = 512 + 128 * (b // 2)
                top, mid = upper[0:8, spot : spot + 128], upper[8:16, spot : spot + 128]
                end = lower[:, spot : spot + 128]
                if b % 2 == 0:
                    mixed = jnp.where(half, top, pltpu.roll(mid, 64, 1))
                else:
                    mixed = jnp.where(half, pltpu.roll(top, 64, 1), mid)
                    end = pltpu.roll(end, 64, 1)
                lanes = slice(128 * b, 128 * b + 128)
                slab = jnp.concatenate(
                    [upper[:, lanes], lower[:, lanes], mixed, end], axis=0
                )
                tri_out[u, 4 * lead + b] = slab.reshape(TRI_TILES, 8, 128).astype(jnp.bfloat16)
            for b in range(0 if step else 1, 4):
                tri_copy(u, 4 * lead + lax.rem(col + b, 4), me).start()
        tri_in[u, me] = tri_out[u, me]
        each_peer(lambda index: tri_copy(u, index, index).wait_recv())
        if u == 0:
            for n in range(6, 9):
                loads[n].wait()

        for t in range(TRI_TILES):
            home = swap_groups(
                [tri_in[u, g, t].astype(jnp.float32) for g in range(GROUPS)], lane8
            )
            for a in range(GROUPS):
                if t < 3:
                    tri[pl.ds(24 * a + 8 * t, 8), :] = home[a]
                elif t == 3:
                    tri[pl.ds(24 * (16 + a % 8) + 8 * (a // 8), 8), :] = home[a]
                elif a < 8:
                    tri[pl.ds(24 * (16 + a) + 16, 8), :] = home[a]

        for t in range(3):
            rows = pl.ds(192 * t, 192)
            tri_norm = norm_rows(
                tri[rows, :], gain[2 * u + 1 : 2 * u + 2, :], bias[2 * u + 1 : 2 * u + 2, :]
            )
            change = jnp.dot(tri_norm, w_out[u], preferred_element_type=jnp.float32)
            if u == 0:
                for s in range(8):
                    across = pl.ds(8 * t + s, SIDE, stride=SIDE)
                    state[pl.ds(192 * t + 24 * s, 24), :] = (
                        pair[across, :] + gates[across, :] * change[24 * s : 24 * s + 24]
                    )
            else:
                state[rows, :] = state[rows, :] + gates[rows, :] * change

    hidden = w_down.shape[0]
    for t in range(3):
        rows = pl.ds(192 * t, 192)
        values = state[rows, :]
        unit = norm_rows(values, gain[4:5, :], bias[4:5, :])
        pre = jnp.dot(unit, w_in[...], preferred_element_type=jnp.float32)
        gate = pre[:, :hidden]
        act = (gate * sigmoid(gate) * pre[:, hidden:]).astype(jnp.bfloat16)
        out[rows, :] = values + jnp.dot(act, w_down[...], preferred_element_type=jnp.float32)
    for u in range(2):
        each_peer(lambda index: edge_copy(u, index, me).wait_send())
        each_peer(lambda index: tri_copy(u, index, me).wait_send())


def split_channels(cols, pair, chain, block_mask, gain, bias, w_proj, w_out, w_in, w_down):
    rows = pair.shape[0] * pair.shape[1]
    vmem, hbm = pl.BlockSpec(memory_space=pltpu.VMEM), pl.BlockSpec(memory_space=pltpu.HBM)
    operands = (
        pair.reshape(rows, 128), chain, block_mask, gain, bias, w_proj, w_out, w_in, w_down
    )
    result = pl.pallas_call(
        functools.partial(kernel, cols),
        out_shape=jax.ShapeDtypeStruct((rows, 128), jnp.float32),
        in_specs=[hbm] * 9,
        out_specs=vmem,
        scratch_shapes=[
            (pltpu.SMEM if n in (1, 2) else pltpu.VMEM)(array.shape, array.dtype)
            for n, array in enumerate(operands)
        ]
        + [
            pltpu.VMEM((GROUPS, 8 * LR_TILES, 128), jnp.float32),
            pltpu.VMEM((rows, 128), jnp.bfloat16),
            pltpu.VMEM((rows, 128), jnp.float32),
            pltpu.VMEM((rows, 128), jnp.float32),
            pltpu.VMEM((rows, 128), jnp.float32),
            pltpu.VMEM((12, 4 * SIDE, 128), jnp.float32),
            pltpu.VMEM((2, GROUPS, LR_TILES, 8, 128), jnp.bfloat16),
            pltpu.VMEM((2, GROUPS, LR_TILES, 8, 128), jnp.bfloat16),
            pltpu.VMEM((2, GROUPS, TRI_TILES, 8, 128), jnp.bfloat16),
            pltpu.VMEM((2, GROUPS, TRI_TILES, 8, 128), jnp.bfloat16),
            pltpu.SemaphoreType.DMA((9,)),
            pltpu.SemaphoreType.DMA((4, GROUPS)),
            pltpu.SemaphoreType.DMA((4, GROUPS)),
        ],
        compiler_params=pltpu.CompilerParams(
            collective_id=0, has_side_effects=True, vmem_limit_bytes=56 * 1024 * 1024
        ),
        cost_estimate=pl.CostEstimate(
            flops=900_000_000, bytes_accessed=2_000_000, transcendentals=1_000_000
        ),
    )(*operands)
    return result.reshape(pair.shape[1], pair.shape[0], 128).swapaxes(0, 1)


def solution(mesh):
    if mesh.shape["row"] == 4 and mesh.shape["col"] == 4:
        body = functools.partial(split_channels, mesh.shape["col"])
    else:
        body = local
    return jax.shard_map(
        body,
        mesh=mesh,
        in_specs=(
            P(("parts", "row"), "col", None),
            P("parts"),
            P("parts", None),
            P(),
            P(),
            P(),
            P(),
            P(),
            P(),
        ),
        out_specs=P(("parts", "row"), "col", None),
        check_vma=False,
    )
```

```python
import functools

import jax
import jax.numpy as jnp
from jax import lax
from jax.experimental import pallas as pl
from jax.experimental.pallas import tpu as pltpu
from jax.sharding import PartitionSpec as P

MASK_TILE = 8
MESH = pl.DeviceIdType.MESH


def broadcast(array, axis, root):
    mine = lax.axis_index(axis) == root
    return lax.psum(jnp.where(mine, array, jnp.zeros_like(array)), axis)


def layer_norm(values, gain, bias):
    center = jnp.mean(values, axis=-1, keepdims=True)
    spread = jnp.mean((values - center) ** 2, axis=-1, keepdims=True)
    return (values - center) * lax.rsqrt(spread + 1e-05) * gain + bias


def project_edges(state, pair_mask, norm_gain, norm_bias, w_proj, update):
    channels = state.shape[2]
    normed = layer_norm(state, norm_gain[2 * update], norm_bias[2 * update]).astype(jnp.bfloat16)
    proj = jnp.dot(normed, w_proj[update], preferred_element_type=jnp.float32)
    left_edge = (
        jax.nn.sigmoid(proj[..., 0:channels]) * proj[..., channels : 2 * channels] * pair_mask
    ).astype(jnp.bfloat16)
    right_edge = (
        jax.nn.sigmoid(proj[..., 2 * channels : 3 * channels])
        * proj[..., 3 * channels : 4 * channels]
        * pair_mask
    ).astype(jnp.bfloat16)
    gating = jax.nn.sigmoid(proj[..., 4 * channels :])
    return (left_edge, right_edge, gating)


def finish_update(state, triangle, gating, norm_gain, norm_bias, w_out, update):
    tri_norm = layer_norm(triangle, norm_gain[2 * update + 1], norm_bias[2 * update + 1]).astype(
        jnp.bfloat16
    )
    return state + gating * jnp.dot(tri_norm, w_out[update], preferred_element_type=jnp.float32)


def local(pair, chain, block_mask, norm_gain, norm_bias, w_proj, w_out, w_trans_in, w_trans_out):
    extent = pair.shape[0]
    row_offset = lax.axis_index("row") * extent
    col_offset = lax.axis_index("col") * extent
    row_chain = lax.dynamic_slice_in_dim(chain, row_offset, extent)
    col_chain = lax.dynamic_slice_in_dim(chain, col_offset, extent)
    expanded = jnp.repeat(jnp.repeat(block_mask, MASK_TILE, axis=0), MASK_TILE, axis=1)
    local_blocks = lax.dynamic_slice(expanded, (row_offset, col_offset), (extent, extent)) > 0
    same_chain = row_chain[:, None] == col_chain[None, :]
    pair_mask = jnp.logical_or(same_chain, local_blocks).astype(jnp.float32)[..., None]
    state = pair
    left_edge, right_edge, gating = project_edges(state, pair_mask, norm_gain, norm_bias, w_proj, 0)
    right_strip = lax.all_gather(right_edge, "col", axis=1, tiled=True)
    mirrored_right = broadcast(right_strip, "row", lax.axis_index("col"))
    partner = mirrored_right
    triangle = jnp.einsum(
        "ikc,jkc->ijc",
        lax.all_gather(left_edge, "col", axis=1, tiled=True),
        partner,
        preferred_element_type=jnp.float32,
    )
    state = finish_update(state, triangle, gating, norm_gain, norm_bias, w_out, 0)
    left_edge, right_edge, gating = project_edges(state, pair_mask, norm_gain, norm_bias, w_proj, 1)
    left_strip = lax.all_gather(left_edge, "row", axis=0, tiled=True)
    mirrored_left = broadcast(left_strip, "col", lax.axis_index("row"))
    partner = mirrored_left
    triangle = jnp.einsum(
        "kic,kjc->ijc",
        partner,
        lax.all_gather(right_edge, "row", axis=0, tiled=True),
        preferred_element_type=jnp.float32,
    )
    state = finish_update(state, triangle, gating, norm_gain, norm_bias, w_out, 1)
    trans_norm = layer_norm(state, norm_gain[4], norm_bias[4]).astype(jnp.bfloat16)
    hidden_pre = jnp.dot(trans_norm, w_trans_in, preferred_element_type=jnp.float32)
    width = w_trans_out.shape[0]
    activated = (jax.nn.silu(hidden_pre[..., :width]) * hidden_pre[..., width:]).astype(
        jnp.bfloat16
    )
    return state + jnp.dot(activated, w_trans_out, preferred_element_type=jnp.float32)


GROUPS = 16
WIDTH = 8
SIDE = 24
LR_TILES = 9
TRI_TILES = 5


def sigmoid(x):
    return 0.5 * jnp.tanh(0.5 * x) + 0.5


def swap_groups(values, lane):
    values = list(values)
    for step in (8, 4, 2, 1):
        low = (lane & (step * WIDTH)) == 0
        for a in range(GROUPS):
            if a & step:
                continue
            first, second = values[a], values[a + step]
            values[a] = jnp.where(low, first, pltpu.roll(second, step * WIDTH, 1))
            values[a + step] = jnp.where(low, pltpu.roll(first, 128 - step * WIDTH, 1), second)
    return values


def norm_rows(x, gain, bias):
    center = jnp.mean(x, axis=-1, keepdims=True)
    off = x - center
    spread = jnp.mean(off * off, axis=-1, keepdims=True)
    return (off * lax.rsqrt(spread + 1e-05) * gain + bias).astype(jnp.bfloat16)


def kernel(
    cols, pair_hbm, chain_hbm, block_hbm, gain_hbm, bias_hbm, proj_hbm, out_hbm, in_hbm, down_hbm,
    out, pair, chain, block_mask, gain, bias, w_proj, w_out, w_in, w_down,
    edges, normed, gates, state, tri, grid, lr_out, lr_in, tri_out, tri_in,
    done, load_sem, send_sem, recv_sem,
):
    row, col = lax.axis_index("row"), lax.axis_index("col")
    me = row * cols + col
    loads = [
        pltpu.make_async_copy(src, dst, load_sem.at[n])
        for n, (src, dst) in enumerate(
            (
                (pair_hbm, pair),
                (chain_hbm, chain),
                (block_hbm, block_mask),
                (gain_hbm, gain),
                (bias_hbm, bias),
                (proj_hbm, w_proj),
                (out_hbm, w_out),
                (in_hbm, w_in),
                (down_hbm, w_down),
            )
        )
    ]
    def place(index):
        return {"row": index // cols, "col": lax.rem(index, cols)}

    barrier = pltpu.get_barrier_semaphore()

    def greet(d, carry):
        pl.semaphore_signal(
            barrier, inc=1, device_id=place(lax.rem(me + d, GROUPS)), device_id_type=MESH
        )
        return carry

    lax.fori_loop(1, GROUPS, greet, 0)
    for load in loads:
        load.start()

    def remote(phase, source, target, index, slot):
        return pltpu.make_async_remote_copy(
            src_ref=source.at[index],
            dst_ref=target.at[slot],
            send_sem=send_sem.at[phase, index],
            recv_sem=recv_sem.at[phase, slot],
            device_id=place(index),
            device_id_type=MESH,
        )

    def edge_copy(u, index, slot):
        return remote(2 * u, lr_out.at[u], lr_in.at[u], index, slot)

    def tri_copy(u, index, slot):
        return remote(2 * u + 1, tri_out.at[u], tri_in.at[u], index, slot)

    def each_peer(action):
        def body(d, carry):
            action(lax.rem(me + d, GROUPS))
            return carry

        lax.fori_loop(1, GROUPS, body, 0)

    sub = lax.broadcasted_iota(jnp.int32, (8, 128), 0)

    def spread_ids(ids):
        rows = []
        for t in range(SIDE // 8):
            v = jnp.full((8, 128), ids[8 * t], jnp.int32)
            for s in range(1, 8):
                v = jnp.where(sub == s, ids[8 * t + s], v)
            rows.append(v)
        return rows

    for n in range(5):
        loads[n].wait()
    row_ids = [chain[row * SIDE + i] for i in range(SIDE)]
    col_ids = [chain[col * SIDE + i] for i in range(SIDE)]
    per_side = SIDE // MASK_TILE
    tiles = [
        [block_mask[row * per_side + a, col * per_side + b] for b in range(per_side)]
        for a in range(per_side)
    ]

    def mask_tile(update, i, t):
        lead, others = (row_ids, spread_cols) if update == 0 else (col_ids, spread_rows)
        tile = tiles[i // 8][t] if update == 0 else tiles[t][i // 8]
        return jnp.where(
            others[t] == lead[i], 1, jnp.full((8, 128), tile, jnp.int32)
        ).astype(jnp.float32)

    spread_rows, spread_cols = spread_ids(row_ids), spread_ids(col_ids)
    lane8 = lax.broadcasted_iota(jnp.int32, (8, 128), 1)
    low96 = lax.broadcasted_iota(jnp.int32, (4 * SIDE, 128), 1) < 64
    same = (lax.broadcasted_iota(jnp.int32, (128, 768), 0) & 7) == (
        lax.broadcasted_iota(jnp.int32, (128, 768), 1) & 7
    )
    fold = jnp.where(
        lax.broadcasted_iota(jnp.int32, (16, 128), 1) // WIDTH
        == lax.broadcasted_iota(jnp.int32, (16, 128), 0),
        1.0,
        0.0,
    ).astype(jnp.bfloat16)
    loads[5].wait()

    for u in range(2):
        origin = pair if u == 0 else state
        for chunk in range(3):
            piece = chunk // 2
            first, lines, depth = ((0, 12, 16), (12, 12, 16), (0, 24, 8))[chunk]
            base = 16 * piece
            values = jnp.concatenate(
                [origin[pl.ds(24 * (first + n) + base, depth), :] for n in range(lines)], axis=0
            )
            unit = norm_rows(values, gain[2 * u : 2 * u + 1, :], bias[2 * u : 2 * u + 1, :])
            normed[pl.ds(192 * chunk, 192), :] = unit
            proj = jnp.dot(unit, w_proj[u, :, 0:512], preferred_element_type=jnp.float32)
            left = sigmoid(proj[:, 0:128]) * proj[:, 128:256]
            right = sigmoid(proj[:, 256:384]) * proj[:, 384:512]
            for n in range(lines):
                i = first + n
                for h in range(depth // 8):
                    mask = mask_tile(u, i, base // 8 + h)
                    rows = pl.ds(48 * piece + depth * (i // 8) + 8 * h, 8)
                    at = n * depth + 8 * h
                    edges[i % 8, rows, :] = left[at : at + 8] * mask
                    edges[8 + i % 8, rows, :] = right[at : at + 8] * mask
            for t in ((), range(6), range(6, LR_TILES))[chunk]:
                rows = pl.ds(8 * t, 8)
                swapped = swap_groups([edges[a, rows, :] for a in range(GROUPS)], lane8)
                for g in range(GROUPS):
                    lr_out[u, g, t] = swapped[g].astype(jnp.bfloat16)
        if u == 0:
            pl.semaphore_wait(barrier, GROUPS - 1)
        each_peer(lambda index: edge_copy(u, index, me).start())

        for chunk in range(3):
            first, lines, depth = ((0, 12, 16), (12, 12, 16), (0, 24, 8))[chunk]
            gate = sigmoid(
                jnp.dot(
                    normed[pl.ds(192 * chunk, 192), :],
                    w_proj[u, :, 512:640],
                    preferred_element_type=jnp.float32,
                )
            )
            for n in range(lines):
                gates[pl.ds(24 * (first + n) + 16 * (chunk // 2), depth), :] = gate[
                    depth * n : depth * n + depth
                ]

        def unpack(source, index):
            if u == 0:
                lead, k = index // 4, lax.rem(index, 4)
            else:
                lead, k = lax.rem(index, 4), index // 4
            at = pl.multiple_of(24 * k, 8)
            slab = source[u, index].astype(jnp.float32).reshape(8 * LR_TILES, 128)
            for t in range(3):
                grid[3 * lead + t, pl.ds(at, 16), :] = slab[16 * t : 16 * t + 16]
                grid[3 * lead + t, pl.ds(at + 16, 8), :] = slab[48 + 8 * t : 56 + 8 * t]

        unpack(lr_out, me)

        def take(d, carry):
            index = lax.rem(me + GROUPS - d, GROUPS)
            edge_copy(u, index, index).wait_recv()
            unpack(lr_in, index)
            return carry

        lax.fori_loop(1, GROUPS, take, 0)

        rights = [
            jnp.where(low96, pltpu.roll(grid[3 * b], 64, 1), grid[3 * b + 1]) for b in range(4)
        ]
        rights += [
            jnp.where(low96, pltpu.roll(grid[3 * b + 2], 64, 1), grid[3 * b + 5]) for b in (0, 2)
        ]
        rights = jnp.concatenate([r.astype(jnp.bfloat16) for r in rights], axis=1)
        half = lane8 < 64
        for step in (2, 1, 3, 0):
            lead = lax.rem(row + step, 4)
            pairs = jnp.where(low96, grid[3 * lead], pltpu.roll(grid[3 * lead + 1], 64, 1))
            product = jnp.dot(
                pairs.T.astype(jnp.bfloat16), rights, preferred_element_type=jnp.float32
            )
            kept = jnp.where(same, product, 0.0).astype(jnp.bfloat16)
            upper = jnp.dot(fold, kept, preferred_element_type=jnp.float32)
            product = jnp.dot(
                grid[3 * lead + 2].T[0:64].astype(jnp.bfloat16),
                rights,
                preferred_element_type=jnp.float32,
            )
            kept = jnp.where(same[0:64], product, 0.0).astype(jnp.bfloat16)
            lower = jnp.dot(fold[0:8, 0:64], kept, preferred_element_type=jnp.float32)
            for b in range(4):
                spot = 512 + 128 * (b // 2)
                top, mid = upper[0:8, spot : spot + 128], upper[8:16, spot : spot + 128]
                end = lower[:, spot : spot + 128]
                if b % 2 == 0:
                    mixed = jnp.where(half, top, pltpu.roll(mid, 64, 1))
                else:
                    mixed = jnp.where(half, pltpu.roll(top, 64, 1), mid)
                    end = pltpu.roll(end, 64, 1)
                lanes = slice(128 * b, 128 * b + 128)
                slab = jnp.concatenate(
                    [upper[:, lanes], lower[:, lanes], mixed, end], axis=0
                )
                tri_out[u, 4 * lead + b] = slab.reshape(TRI_TILES, 8, 128).astype(jnp.bfloat16)
            for b in range(0 if step else 1, 4):
                tri_copy(u, 4 * lead + lax.rem(col + b, 4), me).start()
        tri_in[u, me] = tri_out[u, me]
        each_peer(lambda index: tri_copy(u, index, index).wait_recv())
        if u == 0:
            for n in range(6, 9):
                loads[n].wait()

        for t in range(TRI_TILES):
            home = swap_groups(
                [tri_in[u, g, t].astype(jnp.float32) for g in range(GROUPS)], lane8
            )
            for a in range(GROUPS):
                if t < 3:
                    tri[pl.ds(24 * a + 8 * t, 8), :] = home[a]
                elif t == 3:
                    tri[pl.ds(24 * (16 + a % 8) + 8 * (a // 8), 8), :] = home[a]
                elif a < 8:
                    tri[pl.ds(24 * (16 + a) + 16, 8), :] = home[a]

        for t in range(3):
            rows = pl.ds(192 * t, 192)
            tri_norm = norm_rows(
                tri[rows, :], gain[2 * u + 1 : 2 * u + 2, :], bias[2 * u + 1 : 2 * u + 2, :]
            )
            change = jnp.dot(tri_norm, w_out[u], preferred_element_type=jnp.float32)
            if u == 0:
                for s in range(8):
                    across = pl.ds(8 * t + s, SIDE, stride=SIDE)
                    state[pl.ds(192 * t + 24 * s, 24), :] = (
                        pair[across, :] + gates[across, :] * change[24 * s : 24 * s + 24]
                    )
            else:
                state[rows, :] = state[rows, :] + gates[rows, :] * change

    stores = [
        pltpu.make_async_copy(
            done.at[pl.ds(192 * t, 192)], out.at[pl.ds(192 * t, 192)], load_sem.at[9 + t]
        )
        for t in range(3)
    ]
    hidden = w_down.shape[0]
    for t in range(3):
        rows = pl.ds(192 * t, 192)
        values = state[rows, :]
        unit = norm_rows(values, gain[4:5, :], bias[4:5, :])
        pre = jnp.dot(unit, w_in[...], preferred_element_type=jnp.float32)
        gate = pre[:, :hidden]
        act = (gate * sigmoid(gate) * pre[:, hidden:]).astype(jnp.bfloat16)
        done[rows, :] = values + jnp.dot(act, w_down[...], preferred_element_type=jnp.float32)
        stores[t].start()
    for u in range(2):
        each_peer(lambda index: edge_copy(u, index, me).wait_send())
        each_peer(lambda index: tri_copy(u, index, me).wait_send())
    for store in stores:
        store.wait()


def split_channels(cols, pair, chain, block_mask, gain, bias, w_proj, w_out, w_in, w_down):
    rows = pair.shape[0] * pair.shape[1]
    hbm = pl.BlockSpec(memory_space=pltpu.HBM)
    operands = (
        pair.reshape(rows, 128), chain, block_mask, gain, bias, w_proj, w_out, w_in, w_down
    )
    result = pl.pallas_call(
        functools.partial(kernel, cols),
        out_shape=jax.ShapeDtypeStruct((rows, 128), jnp.float32),
        in_specs=[hbm] * 9,
        out_specs=hbm,
        scratch_shapes=[
            (pltpu.SMEM if n in (1, 2) else pltpu.VMEM)(array.shape, array.dtype)
            for n, array in enumerate(operands)
        ]
        + [
            pltpu.VMEM((GROUPS, 8 * LR_TILES, 128), jnp.float32),
            pltpu.VMEM((rows, 128), jnp.bfloat16),
            pltpu.VMEM((rows, 128), jnp.float32),
            pltpu.VMEM((rows, 128), jnp.float32),
            pltpu.VMEM((rows, 128), jnp.float32),
            pltpu.VMEM((12, 4 * SIDE, 128), jnp.float32),
            pltpu.VMEM((2, GROUPS, LR_TILES, 8, 128), jnp.bfloat16),
            pltpu.VMEM((2, GROUPS, LR_TILES, 8, 128), jnp.bfloat16),
            pltpu.VMEM((2, GROUPS, TRI_TILES, 8, 128), jnp.bfloat16),
            pltpu.VMEM((2, GROUPS, TRI_TILES, 8, 128), jnp.bfloat16),
            pltpu.VMEM((rows, 128), jnp.float32),
            pltpu.SemaphoreType.DMA((12,)),
            pltpu.SemaphoreType.DMA((4, GROUPS)),
            pltpu.SemaphoreType.DMA((4, GROUPS)),
        ],
        compiler_params=pltpu.CompilerParams(
            collective_id=0, has_side_effects=True, vmem_limit_bytes=56 * 1024 * 1024
        ),
        cost_estimate=pl.CostEstimate(
            flops=900_000_000, bytes_accessed=2_000_000, transcendentals=1_000_000
        ),
    )(*operands)
    return result.reshape(pair.shape[1], pair.shape[0], 128).swapaxes(0, 1)


def solution(mesh):
    if mesh.shape["row"] == 4 and mesh.shape["col"] == 4:
        body = functools.partial(split_channels, mesh.shape["col"])
    else:
        body = local
    return jax.shard_map(
        body,
        mesh=mesh,
        in_specs=(
            P(("parts", "row"), "col", None),
            P("parts"),
            P("parts", None),
            P(),
            P(),
            P(),
            P(),
            P(),
            P(),
        ),
        out_specs=P(("parts", "row"), "col", None),
        check_vma=False,
    )
```
